32 devices in a mesh: cx: 4 (over z), cy: 4 (over y, x), orb: 2 (over core).
Axes of the slice: x: 2, y: 2, z: 4, core: 2. Of those that a mesh axis runs over, the one named last changes fastest.
Arguments:
- coeffs: bfloat16 [16, 32, 128, 1024], P('cx', 'cy', None, 'orb'), may hold values from -6 to 6
- occupation: float32 [1024], P('orb'), may hold values from 0.05 to 2
- energies: float32 [1024], P('orb'), may hold values from -1.5 to 0.5
- row_atom: int32 [16, 32, 128], P('cx', 'cy', 'orb'), may hold values from 0 to 7, never falling along the last dimension, each value on 1 to 32 neighbouring positions
- pair_first: int32 [4, 4, 64], P('cx', 'cy'), may hold values from 0 to 31
- pair_second: int32 [4, 4, 64], P('cx', 'cy'), may hold values from 0 to 59, as said below
- pair_count: int32 [4, 4], P('cx', 'cy'), may hold values from 16 to 64, as said below
- deriv_h: bfloat16 [4, 4, 64, 3, 128, 128], P('cx', 'cy', None, None, 'orb'), may hold values from -0.0029296875 to 0.0029296875
- deriv_s: bfloat16 [4, 4, 64, 3, 128, 128], P('cx', 'cy', None, None, 'orb'), may hold values from -0.0029296875 to 0.0029296875
Outputs:
- forces: float32 [3, 16, 32, 8], P(None, 'cx', 'cy')
The draws below stay inside these ranges and needn't reach their ends.
Inputs may be any that keep to these rules, and one draw needn't show every extreme that they name: pair_second indexes the owner's block of clusters extended by one cluster on every side (rows of 10 entries) and lies at most one cluster away from the slot's pair_first cluster in each direction; the pairs of one owner are distinct; slots from pair_count on hold such pairs too and are ignored. `pair_count`: some owners hold exactly 64 live pairs in every draw. `row_atom`: along the last dimension the atom numbers never fall, every atom has 1 to 32 functions.
All inputs are finite; a program needn't handle non-finite values.
Results may differ from the reference program's by a relative error of at most 0.0025.
Values may be sent and summed in bfloat16 or wider, within the bound.
No kernel may reach another device: no remote copies, remote signals or barrier semaphores. Data moves between devices by JAX's collectives and lax.ppermute only.
A program may use at most 192 MiB of HBM per device.

```python
import math
import jax
import jax.numpy as jnp
import numpy as np
from jax import lax

B = 128
NORB = 1024
ATOMS = 8
CLX = 4
CLY = 8
MAXP = 64
GX = 16
GY = 32
N_CX = 4
N_CY = 4


def pair_table(key):
    device_total = N_CX * N_CY
    candidates = CLX * CLY * 9
    device_keys = jax.random.split(key, device_total)

    def one_order(single_key):
        return jax.random.permutation(single_key, candidates)
    orders = jax.vmap(one_order)(device_keys)[:, :MAXP]
    cluster = orders // 9
    offsets = orders % 9
    second_ids = (cluster // CLY + offsets // 3) * (CLY + 2) + cluster % CLY + offsets % 3
    return (cluster.reshape(N_CX, N_CY, MAXP).astype(jnp.int32), second_ids.reshape(N_CX, N_CY, MAXP).astype(jnp.int32))


def draw_pair_first(key, part):
    first_ids, second_ids = pair_table(key)
    return first_ids


def draw_pair_second(key, part):
    first_ids, second_ids = pair_table(key)
    return second_ids


def draw_pair_count(key, part):
    key = jax.random.fold_in(key, 3)
    base_key, busy_key, chosen_key = jax.random.split(key, 3)
    device_total = N_CX * N_CY
    base_counts = jax.random.randint(base_key, (device_total,), MAXP // 4, MAXP // 2 + 1)
    chosen = jax.random.randint(chosen_key, (), 0, device_total)
    busy = (jax.random.randint(busy_key, (device_total,), 0, 8) == 0) | (jnp.arange(device_total) == chosen)
    return jnp.where(busy, MAXP, base_counts).reshape(N_CX, N_CY).astype(jnp.int32)


def level_of(key, shape, cuts, least, top_value):
    def one(dim, blocks):
        steps = jax.random.uniform(jax.random.fold_in(jax.random.fold_in(key, 6), dim), (blocks,), jnp.float32, least / len(cuts), top_value / len(cuts))
        return jnp.repeat(jnp.exp(steps), shape[dim] // blocks).reshape((-1,) + (1,) * (len(shape) - dim - 1))

    loudness = one(*cuts[0])
    for cut in cuts[1:]:
        loudness = loudness * one(*cut)
    return loudness


def length_profile(amount, total, bound, lean):
    weights = [(1 << 20) // math.isqrt(rank ** lean) + 1 for rank in range(2, amount + 1)]
    rest, given = total - bound - (amount - 1), [1] * (amount - 1)
    while rest > 0:
        free = [i for i in range(amount - 1) if given[i] < bound]
        mass, left = sum([weights[i] for i in free]), rest
        for i in free:
            addition = min(bound - given[i], max(1, left * weights[i] // mass), rest)
            given[i] = given[i] + addition
            rest = rest - addition
    return np.array([bound] + given)


def ragged(stream_key, count, total, limit, lean):
    if count == 2:
        one = jax.random.randint(stream_key, (), max(1, total - limit), min(limit, total - 1) + 1)
        return jnp.stack([one, total - one])
    tallies = jnp.asarray(length_profile(count, total, limit, lean), jnp.int32)
    pairs = (count - 1) // 2
    source_of, sink = tallies[1:1 + 2 * pairs:2], tallies[2:2 + 2 * pairs:2]
    room = jnp.minimum(source_of - 1, limit - sink)
    shifted = jax.random.randint(jax.random.fold_in(stream_key, 1), (pairs,), 0, 1 << 20) % (room + 1)
    tallies = tallies.at[1:1 + 2 * pairs:2].set(source_of - shifted).at[2:2 + 2 * pairs:2].set(sink + shifted)
    return tallies[jax.random.permutation(jax.random.fold_in(stream_key, 2), count)]


def bell_draw(key, dims, spread, bound, cuts=(), kind=jnp.bfloat16):
    gain = level_of(key, dims, cuts, -0.22, 0.18) if cuts else 1.0
    array = jax.random.normal(key, dims, jnp.float32) * spread * gain
    return jnp.minimum(jnp.maximum(array, -bound), bound).astype(kind)


def setup_inputs(seed: int = 0) -> dict:
    streams_of = jax.random.split(jax.random.key(seed), 10)
    return {
        "coeffs": bell_draw(streams_of[0], (GX, GY, B, NORB), 1.0, 6.0, ((0, 4), (1, 4), (3, 2))),
        "occupation": jnp.clip(jnp.exp(math.log(2.0) - 3.6888794 * jax.random.uniform(streams_of[1], (NORB,), jnp.float32) ** level_of(streams_of[1], (NORB,), ((0, 2),), -0.2, 0.2)), 0.05, 2.0),
        "energies": jnp.clip(-1.5 + 2.0 * jax.random.uniform(streams_of[2], (NORB,), jnp.float32) ** level_of(streams_of[2], (NORB,), ((0, 2),), -0.2, 0.2), -1.5, 0.5),
        "row_atom": jax.vmap(lambda own: jnp.searchsorted(jnp.cumsum(ragged(own, ATOMS, B, 2 * B // ATOMS, 1)), jnp.arange(B), side="right"))(jax.random.split(streams_of[3], GX * GY)).reshape((GX, GY, B)).astype(jnp.int32),
        "pair_first": draw_pair_first(jax.random.fold_in(streams_of[9], 71), 0),
        "pair_second": draw_pair_second(jax.random.fold_in(streams_of[9], 71), 0),
        "pair_count": draw_pair_count(jax.random.fold_in(streams_of[9], 71), 0),
        "deriv_h": bell_draw(streams_of[7], (N_CX, N_CY, MAXP, 3, B, B), (0.5 / NORB), 0.0029296875, ((0, 4), (1, 4), (4, 2))),
        "deriv_s": bell_draw(streams_of[8], (N_CX, N_CY, MAXP, 3, B, B), (0.5 / NORB), 0.0029296875, ((0, 4), (1, 4), (4, 2))),
    }


def reference(coeffs, occupation, energies, row_atom, pair_first, pair_second, pair_count, deriv_h, deriv_s):
    highest = lax.Precision.HIGHEST

    def device_terms(totals, device):
        block_x = device // N_CY
        block_y = device % N_CY
        first_list = pair_first[block_x, block_y]
        second_list = pair_second[block_x, block_y]
        live_count = pair_count[block_x, block_y]
        row_x = (block_x * CLX + first_list // CLY).astype(jnp.int32)
        row_y = (block_y * CLY + first_list % CLY).astype(jnp.int32)
        col_x = ((block_x * CLX + second_list // (CLY + 2) - 1) % GX).astype(jnp.int32)
        col_y = ((block_y * CLY + second_list % (CLY + 2) - 1) % GY).astype(jnp.int32)
        left_rows = coeffs[row_x, row_y].astype(jnp.float32)
        right_rows = coeffs[col_x, col_y].astype(jnp.float32)
        scaled = right_rows * occupation
        stacked = jnp.concatenate((scaled.astype(jnp.bfloat16), (scaled * energies).astype(jnp.bfloat16)), axis=1).astype(jnp.float32)
        products = jnp.einsum("pmo,pno->pmn", left_rows, stacked, precision=highest)
        grad_h = deriv_h[block_x, block_y].astype(jnp.float32)
        grad_s = deriv_s[block_x, block_y].astype(jnp.float32)
        rowsum = jnp.sum(products[:, None, :, :B] * grad_h - products[:, None, :, B:] * grad_s, axis=3)
        atom_ids = row_atom[row_x, row_y]
        atom_pick = (atom_ids[:, :, None] == jnp.arange(ATOMS, dtype=jnp.int32)).astype(jnp.float32)
        live_mask = (jnp.arange(MAXP, dtype=jnp.int32) < live_count).astype(jnp.float32)
        per_atom = jnp.einsum("pcm,pma->pca", rowsum, atom_pick, precision=highest) * live_mask[:, None, None]
        totals = totals.at[:, row_x, row_y, :].add(jnp.transpose(per_atom, (1, 0, 2)))
        return totals, None

    start_totals = jnp.zeros((3, GX, GY, ATOMS), jnp.float32)
    totals, unused = lax.scan(device_terms, start_totals, jnp.arange(N_CX * N_CY, dtype=jnp.int32))
    return -2.0 * totals
```

```python
import functools

import jax
import jax.numpy as jnp
from jax import lax
from jax.experimental import pallas as pl
from jax.experimental.pallas import tpu as pltpu
from jax.sharding import PartitionSpec as P

ATOMS = 8
RING = 8
ANY = pl.BlockSpec(memory_space=pl.ANY)
SMEM = pl.BlockSpec(memory_space=pltpu.SMEM)
VMEM = pl.BlockSpec(memory_space=pltpu.VMEM)


def shift(cells, axis, step):
    count = lax.axis_size(axis)
    return lax.ppermute(cells, axis, [(i, (i + step) % count) for i in range(count)])


def pair_term(left, right, occ, energy, atoms, grad):
    scaled = right.astype(jnp.float32) * occ
    weights = jnp.concatenate(
        (scaled.astype(jnp.bfloat16), (scaled * energy).astype(jnp.bfloat16)), axis=0
    )
    both = lax.dot_general(
        left, weights, (((1,), (1,)), ((), ())), preferred_element_type=jnp.float32
    )
    basis = right.shape[0]
    density, weighted = both[:, :basis], both[:, basis:]
    terms = jnp.concatenate(
        [
            density * grad(0, c).astype(jnp.float32) - weighted * grad(1, c).astype(jnp.float32)
            for c in range(3)
        ],
        axis=1,
    )
    high = terms.astype(jnp.bfloat16)
    low = (terms - high.astype(jnp.float32)).astype(jnp.bfloat16)
    pick = (lax.broadcasted_iota(jnp.int32, (ATOMS, basis), 0) == atoms).astype(jnp.bfloat16)
    return lax.dot_general(
        jnp.concatenate((pick, pick), axis=1),
        jnp.concatenate((high, low), axis=0),
        (((1,), (0,)), ((), ())),
        preferred_element_type=jnp.float32,
    )


def sort_slots(dims, second, count, lists):
    width_x, width_y, slots = dims
    for k in range(3):
        lists[3 * slots + k] = 0

    def place(s, carry):
        g = second[s]
        gx, gy = g // (width_y + 2), g % (width_y + 2)
        inside_x = jnp.logical_and(gx >= 1, gx <= width_x)
        inside_y = jnp.logical_and(gy >= 1, gy <= width_y)
        stage = jnp.where(inside_x, jnp.where(inside_y, 0, 1), 2)
        used = lists[3 * slots + stage]
        lists[stage * slots + used] = s
        lists[3 * slots + stage] = used + 1
        return carry

    lax.fori_loop(0, count, place, 0)


def stage_body(
    dims, stage, first, second, half, lists, coeffs, rims, grads, occ, energy, atoms, acc, scratch
):
    width_x, width_y, slots = dims
    left_ring, right_ring, grad_ring, sems = scratch
    half_rows = grads[0].shape[2]
    number = lists[3 * slots + stage]

    def grad_copies(s, r):
        out = []
        for kind in range(2):
            for part in range(2):
                out.append(
                    pltpu.make_async_copy(
                        grads[2 * kind + part].at[s],
                        grad_ring.at[r, kind, :, pl.ds(part * half_rows, half_rows), :],
                        sems.at[r, 2 * kind + part],
                    )
                )
        return out

    def left_copies(s, r):
        own = first[s]
        return [
            pltpu.make_async_copy(
                coeffs.at[own, pl.ds(pl.multiple_of(part * half_rows, half_rows), half_rows)],
                left_ring.at[r, pl.ds(place * half_rows, half_rows)],
                sems.at[r, 4 + place],
            )
            for place, part in enumerate((half, 1 - half))
        ]

    def right_copy(source, r):
        return pltpu.make_async_copy(source, right_ring.at[r], sems.at[r, 6])

    def start(i):
        s = lists[stage * slots + i]
        r = lax.rem(i, RING)
        g = second[s]
        gx, gy = g // (width_y + 2) - 1, g % (width_y + 2) - 1
        if stage == 0:
            right_copy(coeffs.at[gx * width_y + gy], r).start()
        elif stage == 1:
            for side, rim in enumerate(rims):

                @pl.when((gy < 0) == (side == 0))
                def _():
                    right_copy(rim.at[gx], r).start()
        else:
            row = (gx > 0).astype(jnp.int32)
            low_edge, high_edge, low_mid, high_mid, low_corner, high_corner = rims
            at_edge = jnp.logical_or(gy == 0, gy == width_y - 1)
            outside = jnp.logical_or(gy < 0, gy >= width_y)
            inner = jnp.logical_not(jnp.logical_or(at_edge, outside))
            for side, edge, mid, corner in (
                (0, low_edge, low_mid, low_corner),
                (1, high_edge, high_mid, high_corner),
            ):
                here = row == side

                @pl.when(jnp.logical_and(here, at_edge))
                def _():
                    right_copy(edge.at[(gy > 0).astype(jnp.int32)], r).start()

                @pl.when(jnp.logical_and(here, inner))
                def _():
                    right_copy(mid.at[gy - 1], r).start()

                @pl.when(jnp.logical_and(outside, (gy < 0) == (side == 0)))
                def _():
                    right_copy(corner.at[row], r).start()

        for copy in left_copies(s, r) + grad_copies(s, r):
            copy.start()

    def begin(i, carry):
        start(i)
        return carry

    lax.fori_loop(0, jnp.minimum(number, RING - 1), begin, 0)

    def visit(i, carry):
        @pl.when(i + RING - 1 < number)
        def _():
            start(i + RING - 1)

        s = lists[stage * slots + i]
        r = lax.rem(i, RING)
        own = first[s]
        right_copy(coeffs.at[0], r).wait()
        for copy in left_copies(s, r) + grad_copies(s, r):
            copy.wait()
        acc[own] += pair_term(
            left_ring[r],
            right_ring[r],
            occ[...],
            energy[...],
            atoms[pl.ds(own, 1), :],
            lambda kind, c: grad_ring[r, kind, c],
        )
        return carry

    lax.fori_loop(0, number, visit, 0)


def own_kernel(
    dims, first, second, meta, coeffs, gh, gh2, gs, gs2, occ, energy, atoms, acc, lists, *scratch
):
    acc[...] = jnp.zeros_like(acc)
    sort_slots(dims, second, meta[0], lists)
    stage_body(
        dims, 0, first, second, meta[1], lists, coeffs, (), (gh, gh2, gs, gs2), occ, energy, atoms,
        acc, scratch,
    )


def rim_kernel(
    dims, stage, rim_count, first, second, meta, lists, coeffs, gh, gh2, gs, gs2, occ, energy,
    atoms, before, *rest
):
    rims, out, scratch = rest[:rim_count], rest[rim_count], rest[rim_count + 1 :]
    if stage == 1:
        acc = out
    else:
        acc, scratch = scratch[-1], scratch[:-1]
    acc[...] = before[...]
    stage_body(
        dims, stage, first, second, meta[1], lists, coeffs, rims, (gh, gh2, gs, gs2), occ, energy,
        atoms, acc, scratch,
    )
    if stage == 2:
        basis = atoms.shape[1]
        for c in range(3):
            out[c] = -2.0 * jnp.sum(acc[:, :, c * basis : (c + 1) * basis], axis=2)


def per_device(
    coeffs, occupation, energies, row_atom, pair_first, pair_second, pair_count, deriv_h, deriv_s
):
    width_x, width_y, basis, columns = coeffs.shape
    half_rows = row_atom.shape[2]
    local = width_x * width_y
    slots = pair_first.shape[2]
    dims = (width_x, width_y, slots)

    edge_pair = jnp.stack((coeffs[:, 0], coeffs[:, width_y - 1]), axis=1)
    low_edge = shift(edge_pair[width_x - 1], "cx", 1)
    high_edge = shift(edge_pair[0], "cx", -1)
    low_mid = shift(coeffs[width_x - 1, 1 : width_y - 1], "cx", 1)
    high_mid = shift(coeffs[0, 1 : width_y - 1], "cx", -1)
    low_side = shift(edge_pair[:, 1], "cy", 1)
    high_side = shift(edge_pair[:, 0], "cy", -1)
    low_corner = shift(jnp.stack((low_edge[1], high_edge[1])), "cy", 1)
    high_corner = shift(jnp.stack((low_edge[0], high_edge[0])), "cy", -1)

    grad_h = deriv_h.reshape(slots, 3, half_rows, basis)
    grad_s = deriv_s.reshape(slots, 3, half_rows, basis)
    grads = (grad_h, shift(grad_h, "orb", 1), grad_s, shift(grad_s, "orb", 1))
    atoms_own = row_atom.reshape(local, half_rows)
    atoms = jnp.concatenate((atoms_own, shift(atoms_own, "orb", 1)), axis=1)

    flat = coeffs.reshape(local, basis, columns)
    first, second = pair_first.reshape(slots), pair_second.reshape(slots)
    meta = jnp.stack((pair_count.reshape(()), lax.axis_index("orb").astype(jnp.int32)))
    occ, energy = occupation.reshape(1, columns), energies.reshape(1, columns)

    scratch = [
        pltpu.VMEM((RING, basis, columns), jnp.bfloat16),
        pltpu.VMEM((RING, basis, columns), jnp.bfloat16),
        pltpu.VMEM((RING, 2, 3, basis, basis), jnp.bfloat16),
        pltpu.SemaphoreType.DMA((RING, 7)),
    ]
    acc_shape = jax.ShapeDtypeStruct((local, ATOMS, 3 * basis), jnp.float32)
    list_shape = jax.ShapeDtypeStruct((3 * slots + 8,), jnp.int32)
    params = pltpu.CompilerParams(vmem_limit_bytes=24 * 1024 * 1024)

    def cost(share):
        pairs = int(slots * share)
        return pl.CostEstimate(
            flops=pairs * basis * 2 * basis * columns * 2,
            bytes_accessed=pairs * 2 * (2 * basis * columns + 6 * basis * basis),
            transcendentals=0,
        )

    acc, lists = pl.pallas_call(
        functools.partial(own_kernel, dims),
        out_shape=(acc_shape, list_shape),
        in_specs=[SMEM] * 3 + [ANY] * 5 + [VMEM] * 3,
        out_specs=(VMEM, SMEM),
        scratch_shapes=scratch,
        compiler_params=params,
        cost_estimate=cost(0.75),
    )(first, second, meta, flat, *grads, occ, energy, atoms)
    for stage, rims, out_shape in (
        (1, (low_side, high_side), acc_shape),
        (
            2,
            (low_edge, high_edge, low_mid, high_mid, low_corner, high_corner),
            jax.ShapeDtypeStruct((3, local, ATOMS), jnp.float32),
        ),
    ):
        acc = pl.pallas_call(
            functools.partial(rim_kernel, dims, stage, len(rims)),
            out_shape=out_shape,
            in_specs=[SMEM] * 4 + [ANY] * 5 + [VMEM] * 4 + [ANY] * len(rims),
            out_specs=VMEM,
            scratch_shapes=scratch
            + ([pltpu.VMEM(acc_shape.shape, jnp.float32)] if stage == 2 else []),
            compiler_params=params,
            cost_estimate=cost(0.15),
        )(first, second, meta, lists, flat, *grads, occ, energy, atoms, acc, *rims)
    return lax.psum(acc, "orb").reshape(3, width_x, width_y, ATOMS)


def solution(mesh):
    return jax.shard_map(
        per_device,
        mesh=mesh,
        in_specs=(
            P("cx", "cy", None, "orb"),
            P("orb"),
            P("orb"),
            P("cx", "cy", "orb"),
            P("cx", "cy", None),
            P("cx", "cy", None),
            P("cx", "cy"),
            P("cx", "cy", None, None, "orb", None),
            P("cx", "cy", None, None, "orb", None),
        ),
        out_specs=P(None, "cx", "cy", None),
        check_vma=False,
    )
```

```python
import functools

import jax
import jax.numpy as jnp
from jax import lax
from jax.experimental import pallas as pl
from jax.experimental.pallas import tpu as pltpu
from jax.sharding import PartitionSpec as P

ATOMS = 8
GROUP = 4
SMEM = pl.BlockSpec(memory_space=pltpu.SMEM)
VMEM = pl.BlockSpec(memory_space=pltpu.VMEM)


def shift(cells, axis, step):
    count = lax.axis_size(axis)
    return lax.ppermute(cells, axis, [(i, (i + step) % count) for i in range(count)])


def pair_terms(pairs, occ, energy):
    products = []
    for left, right, _, _ in pairs:
        scaled = right.astype(jnp.float32) * occ
        weights = jnp.concatenate(
            (scaled.astype(jnp.bfloat16), (scaled * energy).astype(jnp.bfloat16)), axis=0
        )
        products.append(
            lax.dot_general(
                left, weights, (((1,), (1,)), ((), ())), preferred_element_type=jnp.float32
            )
        )
    parts = []
    for both, (_, right, grad, atoms) in zip(products, pairs):
        basis = right.shape[0]
        density, weighted = both[:, :basis], both[:, basis:]
        terms = jnp.concatenate(
            [
                density * grad(0, c).astype(jnp.float32)
                - weighted * grad(1, c).astype(jnp.float32)
                for c in range(3)
            ],
            axis=1,
        )
        high = terms.astype(jnp.bfloat16)
        low = (terms - high.astype(jnp.float32)).astype(jnp.bfloat16)
        pick = (lax.broadcasted_iota(jnp.int32, (ATOMS, basis), 0) == atoms).astype(jnp.bfloat16)
        parts.append(
            lax.dot_general(
                jnp.concatenate((pick, pick), axis=1),
                jnp.concatenate((high, low), axis=0),
                (((1,), (0,)), ((), ())),
                preferred_element_type=jnp.float32,
            )
        )
    return parts


def sort_kernel(dims, second, meta, lists):
    width_x, width_y, slots = dims
    for k in range(3):
        lists[6 * slots + k] = 0

    def place(s, carry):
        g = second[s]
        gx, gy = g // (width_y + 2) - 1, g % (width_y + 2) - 1
        inside_x = jnp.logical_and(gx >= 0, gx < width_x)
        inside_y = jnp.logical_and(gy >= 0, gy < width_y)
        middle = jnp.logical_and(gy >= 1, gy < width_y - 1)
        row = (gx > 0).astype(jnp.int32)
        column = (gy > 0).astype(jnp.int32)
        stage = jnp.where(
            inside_x, jnp.where(inside_y, 0, 1), jnp.where(middle, 2, 1)
        )
        spot = jnp.where(
            inside_x,
            jnp.where(inside_y, gx * width_y + gy, column * width_x + gx),
            jnp.where(
                middle,
                row * (width_y - 2) + gy - 1,
                2 * width_x + jnp.where(inside_y, 2 * row + column, 4 + 2 * column + row),
            ),
        )
        used = lists[6 * slots + stage]
        lists[stage * slots + used] = s
        lists[(3 + stage) * slots + used] = spot
        lists[6 * slots + stage] = used + 1
        return carry

    lax.fori_loop(0, meta[0], place, 0)


def stage_body(dims, stage, right, first, half, lists, coeffs, grads, occ, energy, atoms, acc):
    slots = dims[2]
    half_rows = grads[0].shape[2]
    number = lists[6 * slots + stage]
    offsets = [pl.multiple_of(part * half_rows, half_rows) for part in (half, 1 - half)]

    def visit(i, carry):
        pairs, targets = [], []
        for q in range(GROUP):
            entry = i * GROUP + q
            place = jnp.minimum(entry, number - 1)
            s = lists[stage * slots + place]
            own = first[s]
            left = jnp.concatenate(
                [coeffs[own, pl.ds(offset, half_rows), :] for offset in offsets], axis=0
            )

            def grad(kind, c, s=s):
                return jnp.concatenate(
                    (grads[2 * kind][s, c], grads[2 * kind + 1][s, c]), axis=0
                )

            pairs.append(
                (
                    left,
                    right(lists[(3 + stage) * slots + place]),
                    grad,
                    atoms[pl.ds(own, 1), :],
                )
            )
            targets.append((own, entry < number))
        for (own, live), part in zip(targets, pair_terms(pairs, occ[...], energy[...])):
            acc[own] += jnp.where(live, part, 0.0)
        return carry

    lax.fori_loop(0, (number + GROUP - 1) // GROUP, visit, 0)


def own_kernel(dims, first, meta, lists, coeffs, gh, gh2, gs, gs2, occ, energy, atoms, acc):
    acc[...] = jnp.zeros_like(acc)
    stage_body(
        dims, 0, lambda spot: coeffs[spot], first, meta[1], lists, coeffs, (gh, gh2, gs, gs2), occ,
        energy, atoms, acc,
    )


def side_kernel(
    dims, first, meta, lists, coeffs, gh, gh2, gs, gs2, occ, energy, atoms, before, *rest
):
    rims, acc, cells, sems = rest[:-3], rest[-3], rest[-2], rest[-1]
    copies, start = [], 0
    for k, rim in enumerate(rims):
        size = rim.shape[0]
        copies.append(pltpu.make_async_copy(rim, cells.at[pl.ds(start, size)], sems.at[k]))
        start += size
    for copy in copies:
        copy.start()
    acc[...] = before[...]
    for copy in copies:
        copy.wait()
    stage_body(
        dims, 1, lambda spot: cells[spot], first, meta[1], lists, coeffs, (gh, gh2, gs, gs2), occ,
        energy, atoms, acc,
    )


def last_kernel(
    dims, first, meta, lists, coeffs, gh, gh2, gs, gs2, occ, energy, atoms, before, low, high, out,
    acc,
):
    acc[...] = before[...]
    width = low.shape[0]

    def right(spot):
        up = spot >= width
        return jnp.where(
            up, high[jnp.maximum(spot - width, 0)], low[jnp.minimum(spot, width - 1)]
        )

    stage_body(
        dims, 2, right, first, meta[1], lists, coeffs, (gh, gh2, gs, gs2), occ, energy, atoms, acc
    )
    basis = atoms.shape[1]
    for c in range(3):
        out[c] = -2.0 * jnp.sum(acc[:, :, c * basis : (c + 1) * basis], axis=2)


def per_device(
    coeffs, occupation, energies, row_atom, pair_first, pair_second, pair_count, deriv_h, deriv_s
):
    width_x, width_y, basis, columns = coeffs.shape
    half_rows = row_atom.shape[2]
    local = width_x * width_y
    slots = pair_first.shape[2]
    dims = (width_x, width_y, slots)

    edge_pair = jnp.stack((coeffs[:, 0], coeffs[:, width_y - 1]), axis=1)
    low_edge = shift(edge_pair[width_x - 1], "cx", 1)
    high_edge = shift(edge_pair[0], "cx", -1)
    low_mid = shift(coeffs[width_x - 1, 1 : width_y - 1], "cx", 1)
    high_mid = shift(coeffs[0, 1 : width_y - 1], "cx", -1)
    low_side = shift(edge_pair[:, 1], "cy", 1)
    high_side = shift(edge_pair[:, 0], "cy", -1)
    low_corner = shift(jnp.stack((low_edge[1], high_edge[1])), "cy", 1)
    high_corner = shift(jnp.stack((low_edge[0], high_edge[0])), "cy", -1)

    grad_h = deriv_h.reshape(slots, 3, half_rows, basis)
    grad_s = deriv_s.reshape(slots, 3, half_rows, basis)
    grads = (grad_h, shift(grad_h, "orb", 1), grad_s, shift(grad_s, "orb", 1))
    atoms_own = row_atom.reshape(local, half_rows)
    atoms = jnp.concatenate((atoms_own, shift(atoms_own, "orb", 1)), axis=1)

    flat = coeffs.reshape(local, basis, columns)
    first, second = pair_first.reshape(slots), pair_second.reshape(slots)
    meta = jnp.stack((pair_count.reshape(()), lax.axis_index("orb").astype(jnp.int32)))
    occ, energy = occupation.reshape(1, columns), energies.reshape(1, columns)

    acc_shape = jax.ShapeDtypeStruct((local, ATOMS, 3 * basis), jnp.float32)
    params = pltpu.CompilerParams(vmem_limit_bytes=16 * 1024 * 1024)

    def cost(share):
        pairs = int(slots * share)
        return pl.CostEstimate(
            flops=pairs * basis * 2 * basis * columns * 2,
            bytes_accessed=pairs * 2 * (2 * basis * columns + 6 * basis * basis),
            transcendentals=0,
        )

    lists = pl.pallas_call(
        functools.partial(sort_kernel, dims),
        out_shape=jax.ShapeDtypeStruct((6 * slots + 8,), jnp.int32),
        in_specs=[SMEM] * 2,
        out_specs=SMEM,
    )(second, meta)
    common = (first, meta, lists, flat, *grads, occ, energy, atoms)
    common_specs = [SMEM] * 3 + [VMEM] * 8
    acc = pl.pallas_call(
        functools.partial(own_kernel, dims),
        out_shape=acc_shape,
        in_specs=common_specs,
        out_specs=VMEM,
        compiler_params=params,
        cost_estimate=cost(0.75),
    )(*common)
    rims = (low_side, high_side, low_edge, high_edge, low_corner, high_corner)
    acc = pl.pallas_call(
        functools.partial(side_kernel, dims),
        out_shape=acc_shape,
        in_specs=common_specs + [VMEM] * (1 + len(rims)),
        out_specs=VMEM,
        scratch_shapes=[
            pltpu.VMEM((sum(rim.shape[0] for rim in rims), basis, columns), jnp.bfloat16),
            pltpu.SemaphoreType.DMA((len(rims),)),
        ],
        compiler_params=params,
        cost_estimate=cost(0.15),
    )(*common, acc, *rims)
    out = pl.pallas_call(
        functools.partial(last_kernel, dims),
        out_shape=jax.ShapeDtypeStruct((3, local, ATOMS), jnp.float32),
        in_specs=common_specs + [VMEM] * 3,
        out_specs=VMEM,
        scratch_shapes=[pltpu.VMEM(acc_shape.shape, jnp.float32)],
        compiler_params=params,
        cost_estimate=cost(0.1),
    )(*common, acc, low_mid, high_mid)
    return lax.psum(out, "orb").reshape(3, width_x, width_y, ATOMS)


def solution(mesh):
    return jax.shard_map(
        per_device,
        mesh=mesh,
        in_specs=(
            P("cx", "cy", None, "orb"),
            P("orb"),
            P("orb"),
            P("cx", "cy", "orb"),
            P("cx", "cy", None),
            P("cx", "cy", None),
            P("cx", "cy"),
            P("cx", "cy", None, None, "orb", None),
            P("cx", "cy", None, None, "orb", None),
        ),
        out_specs=P(None, "cx", "cy", None),
        check_vma=False,
    )
```

```python
import functools

import jax
import jax.numpy as jnp
from jax import lax
from jax.experimental import pallas as pl
from jax.experimental.pallas import tpu as pltpu
from jax.sharding import PartitionSpec as P

ATOMS = 8
GROUP = 4
CHUNK = 8
ANY = pl.BlockSpec(memory_space=pl.ANY)
SMEM = pl.BlockSpec(memory_space=pltpu.SMEM)
VMEM = pl.BlockSpec(memory_space=pltpu.VMEM)


def shift(cells, axis, step):
    count = lax.axis_size(axis)
    return lax.ppermute(cells, axis, [(i, (i + step) % count) for i in range(count)])


def after(cells, *others):
    return lax.optimization_barrier((cells, *others))[0]


def pair_terms(pairs, occ, energy):
    products = []
    for left, right, _, _ in pairs:
        scaled = right.astype(jnp.float32) * occ
        weights = jnp.concatenate(
            (scaled.astype(jnp.bfloat16), (scaled * energy).astype(jnp.bfloat16)), axis=0
        )
        products.append(
            lax.dot_general(
                left, weights, (((1,), (1,)), ((), ())), preferred_element_type=jnp.float32
            )
        )
    parts = []
    for both, (_, right, grad, atoms) in zip(products, pairs):
        basis = right.shape[0]
        density, weighted = both[:, :basis], both[:, basis:]
        terms = jnp.concatenate(
            [
                density * grad(0, c).astype(jnp.float32)
                - weighted * grad(1, c).astype(jnp.float32)
                for c in range(3)
            ],
            axis=1,
        )
        high = terms.astype(jnp.bfloat16)
        low = (terms - high.astype(jnp.float32)).astype(jnp.bfloat16)
        pick = (lax.broadcasted_iota(jnp.int32, (ATOMS, basis), 0) == atoms).astype(jnp.bfloat16)
        parts.append(
            lax.dot_general(
                jnp.concatenate((pick, pick), axis=1),
                jnp.concatenate((high, low), axis=0),
                (((1,), (0,)), ((), ())),
                preferred_element_type=jnp.float32,
            )
        )
    return parts


def sort_kernel(dims, first, second, meta, table):
    width_x, width_y, slots = dims
    tail = 9 * slots
    for k in range(3):
        table[tail + k] = 0
    table[tail + 3] = meta[1]
    table[tail + 4] = meta[0]

    def place(s, carry):
        g = second[s]
        gx, gy = g // (width_y + 2) - 1, g % (width_y + 2) - 1
        inside_x = jnp.logical_and(gx >= 0, gx < width_x)
        inside_y = jnp.logical_and(gy >= 0, gy < width_y)
        at_end = jnp.logical_or(gy == 0, gy == width_y - 1)
        row = (gx > 0).astype(jnp.int32)
        column = (gy > 0).astype(jnp.int32)
        stage = jnp.where(inside_x, jnp.where(inside_y, 0, 1), jnp.where(at_end, 1, 2))
        spot = jnp.where(
            inside_x,
            jnp.where(inside_y, gx * width_y + gy, column * width_x + gx),
            jnp.where(
                inside_y,
                jnp.where(at_end, 2 * width_x + 2 * row + column, row * (width_y - 2) + gy - 1),
                2 * (width_y - 2) + 2 * column + row,
            ),
        )
        used = table[tail + stage]
        base = stage * 3 * slots + used
        table[base] = s
        table[base + slots] = first[s]
        table[base + 2 * slots] = spot
        table[tail + stage] = used + 1
        return carry

    lax.fori_loop(0, meta[0], place, 0)


def stage_body(
    dims, stage, right, table, coeffs, grads, occ, energy, atoms, acc, ready=lambda slot, done: done
):
    slots = dims[2]
    half_rows = grads[0].shape[2]
    number, half = table[9 * slots + stage], table[9 * slots + 3]
    offsets = [pl.multiple_of(part * half_rows, half_rows) for part in (half, 1 - half)]

    def visit(i, done):
        final = jnp.minimum(i * GROUP + GROUP - 1, number - 1)
        done = ready(table[stage * 3 * slots + final], done)
        pairs, targets = [], []
        for q in range(GROUP):
            entry = i * GROUP + q
            base = stage * 3 * slots + jnp.minimum(entry, number - 1)
            s, own, spot = table[base], table[base + slots], table[base + 2 * slots]
            left = jnp.concatenate(
                [coeffs[own, pl.ds(offset, half_rows), :] for offset in offsets], axis=0
            )

            def grad(kind, c, s=s):
                return jnp.concatenate(
                    (grads[2 * kind][s, c], grads[2 * kind + 1][s, c]), axis=0
                )

            pairs.append((left, right(spot), grad, atoms[pl.ds(own, 1), :]))
            targets.append((own, entry < number))
        for (own, live), part in zip(targets, pair_terms(pairs, occ[...], energy[...])):
            acc[own] += jnp.where(live, part, 0.0)
        return done

    return lax.fori_loop(0, (number + GROUP - 1) // GROUP, visit, 0)


def own_kernel(
    dims, table, coeffs, gh, gs, gh_far, gs_far, occ, energy, atoms, acc, gh2, gs2, sems
):
    slots = dims[2]
    chunks = (table[9 * slots + 4] + CHUNK - 1) // CHUNK

    def copies(k):
        part = pl.ds(pl.multiple_of(k * CHUNK, CHUNK), CHUNK)
        return [
            pltpu.make_async_copy(far.at[part], near.at[part], sems.at[k, n])
            for n, (far, near) in enumerate(((gh_far, gh2), (gs_far, gs2)))
        ]

    def start(k, carry):
        for copy in copies(k):
            copy.start()
        return carry

    def wait(k, carry):
        for copy in copies(k):
            copy.wait()
        return carry

    def ready(slot, done):
        need = jnp.maximum(slot // CHUNK + 1, done)
        lax.fori_loop(done, need, wait, 0)
        return need

    lax.fori_loop(0, chunks, start, 0)
    acc[...] = jnp.zeros_like(acc)
    done = stage_body(
        dims, 0, lambda spot: coeffs[spot], table, coeffs, (gh, gh2, gs, gs2), occ, energy, atoms,
        acc, ready,
    )
    lax.fori_loop(done, chunks, wait, 0)


def side_kernel(
    dims, table, coeffs, gh, gh2, gs, gs2, occ, energy, atoms, before, *rest
):
    rims, acc, cells, sems = rest[:-3], rest[-3], rest[-2], rest[-1]
    copies, start = [], 0
    for k, rim in enumerate(rims):
        size = rim.shape[0]
        copies.append(pltpu.make_async_copy(rim, cells.at[pl.ds(start, size)], sems.at[k]))
        start += size
    for copy in copies:
        copy.start()
    acc[...] = before[...]
    for copy in copies:
        copy.wait()
    stage_body(
        dims, 1, lambda spot: cells[spot], table, coeffs, (gh, gh2, gs, gs2), occ, energy, atoms, acc,
    )


def last_kernel(
    dims, table, coeffs, gh, gh2, gs, gs2, occ, energy, atoms, before, *rest
):
    rims, out, acc = rest[:-2], rest[-2], rest[-1]
    acc[...] = before[...]

    def right(spot):
        start, cell = 0, None
        for rim in rims:
            size = rim.shape[0]
            here = rim[jnp.clip(spot - start, 0, size - 1)]
            cell = here if cell is None else jnp.where(spot >= start, here, cell)
            start += size
        return cell

    stage_body(
        dims, 2, right, table, coeffs, (gh, gh2, gs, gs2), occ, energy, atoms, acc
    )
    basis = atoms.shape[1]
    for c in range(3):
        out[c] = -2.0 * jnp.sum(acc[:, :, c * basis : (c + 1) * basis], axis=2)


def per_device(
    coeffs, occupation, energies, row_atom, pair_first, pair_second, pair_count, deriv_h, deriv_s
):
    width_x, width_y, basis, columns = coeffs.shape
    half_rows = row_atom.shape[2]
    local = width_x * width_y
    slots = pair_first.shape[2]
    dims = (width_x, width_y, slots)

    grad_h = deriv_h.reshape(slots, 3, half_rows, basis)
    grad_s = deriv_s.reshape(slots, 3, half_rows, basis)
    grad_h_far, grad_s_far = shift(grad_h, "orb", 1), shift(grad_s, "orb", 1)
    low_edge = shift(coeffs[width_x - 1, :: width_y - 1], "cx", 1)
    high_edge = shift(coeffs[0, :: width_y - 1], "cx", -1)
    low_mid = shift(coeffs[width_x - 1, 1 : width_y - 1], "cx", 1)
    low_side = shift(after(coeffs[:, width_y - 1], low_edge), "cy", 1)
    high_side = shift(after(coeffs[:, 0], high_edge), "cy", -1)
    high_mid = shift(coeffs[0, 1 : width_y - 1], "cx", -1)
    low_corner = shift(jnp.stack((low_edge[1], high_edge[1])), "cy", 1)
    high_corner = shift(jnp.stack((low_edge[0], high_edge[0])), "cy", -1)

    half = lax.axis_index("orb")
    atoms_own = row_atom.reshape(local, half_rows)
    atoms_all = lax.all_gather(atoms_own, "orb", axis=0)
    atoms = jnp.concatenate(
        (atoms_own, jnp.where(half == 0, atoms_all[1], atoms_all[0])), axis=1
    )

    flat = coeffs.reshape(local, basis, columns)
    first, second = pair_first.reshape(slots), pair_second.reshape(slots)
    meta = jnp.stack((pair_count.reshape(()), half.astype(jnp.int32)))
    occ, energy = occupation.reshape(1, columns), energies.reshape(1, columns)

    acc_shape = jax.ShapeDtypeStruct((local, ATOMS, 3 * basis), jnp.float32)
    params = pltpu.CompilerParams(vmem_limit_bytes=6 * 1024 * 1024)

    def cost(share):
        pairs = int(slots * share)
        return pl.CostEstimate(
            flops=pairs * basis * 2 * basis * columns * 2,
            bytes_accessed=pairs * 2 * (2 * basis * columns + 6 * basis * basis),
            transcendentals=0,
        )

    table = pl.pallas_call(
        functools.partial(sort_kernel, dims),
        out_shape=jax.ShapeDtypeStruct((9 * slots + 8,), jnp.int32),
        in_specs=[SMEM] * 3,
        out_specs=SMEM,
        compiler_params=pltpu.CompilerParams(vmem_limit_bytes=1024 * 1024),
    )(first, second, meta)
    acc, grad_h2, grad_s2 = pl.pallas_call(
        functools.partial(own_kernel, dims),
        out_shape=(
            acc_shape,
            jax.ShapeDtypeStruct(grad_h.shape, grad_h.dtype),
            jax.ShapeDtypeStruct(grad_s.shape, grad_s.dtype),
        ),
        in_specs=[SMEM] + [VMEM] * 3 + [ANY] * 2 + [VMEM] * 3,
        out_specs=(VMEM, VMEM, VMEM),
        scratch_shapes=[pltpu.SemaphoreType.DMA((slots // CHUNK, 2))],
        compiler_params=params,
        cost_estimate=cost(0.75),
    )(table, flat, grad_h, grad_s, grad_h_far, grad_s_far, occ, energy, atoms)
    common = (table, flat, grad_h, grad_h2, grad_s, grad_s2, occ, energy, atoms)
    common_specs = [SMEM] + [VMEM] * 8
    rims = (low_side, high_side, low_edge, high_edge)
    acc = pl.pallas_call(
        functools.partial(side_kernel, dims),
        out_shape=acc_shape,
        in_specs=common_specs + [VMEM] * (1 + len(rims)),
        out_specs=VMEM,
        scratch_shapes=[
            pltpu.VMEM((sum(rim.shape[0] for rim in rims), basis, columns), jnp.bfloat16),
            pltpu.SemaphoreType.DMA((len(rims),)),
        ],
        compiler_params=params,
        cost_estimate=cost(0.15),
    )(*common, acc, *rims)
    out = pl.pallas_call(
        functools.partial(last_kernel, dims),
        out_shape=jax.ShapeDtypeStruct((3, local, ATOMS), jnp.float32),
        in_specs=common_specs + [VMEM] * 5,
        out_specs=VMEM,
        scratch_shapes=[pltpu.VMEM(acc_shape.shape, jnp.float32)],
        compiler_params=params,
        cost_estimate=cost(0.1),
    )(*common, acc, low_mid, high_mid, low_corner, high_corner)
    total = out + shift(out, "orb", 1)
    return total.reshape(3, width_x, width_y, ATOMS)


def solution(mesh):
    return jax.shard_map(
        per_device,
        mesh=mesh,
        in_specs=(
            P("cx", "cy", None, "orb"),
            P("orb"),
            P("orb"),
            P("cx", "cy", "orb"),
            P("cx", "cy", None),
            P("cx", "cy", None),
            P("cx", "cy"),
            P("cx", "cy", None, None, "orb", None),
            P("cx", "cy", None, None, "orb", None),
        ),
        out_specs=P(None, "cx", "cy", None),
        check_vma=False,
    )
```

```python
import functools

import jax
import jax.numpy as jnp
from jax import lax
from jax.experimental import pallas as pl
from jax.experimental.pallas import tpu as pltpu
from jax.sharding import PartitionSpec as P

ATOMS = 8
GROUP = 4
CHUNK = 8
ANY = pl.BlockSpec(memory_space=pl.ANY)
SMEM = pl.BlockSpec(memory_space=pltpu.SMEM)
VMEM = pl.BlockSpec(memory_space=pltpu.VMEM)


def shift(cells, axis, step):
    count = lax.axis_size(axis)
    return lax.ppermute(cells, axis, [(i, (i + step) % count) for i in range(count)])


def after(cells, *others):
    return lax.optimization_barrier((cells, *others))[0]


def pair_terms(pairs, occ, energy):
    products = []
    for left, right, _, _ in pairs:
        scaled = right.astype(jnp.float32) * occ
        weights = jnp.concatenate(
            (scaled.astype(jnp.bfloat16), (scaled * energy).astype(jnp.bfloat16)), axis=0
        )
        products.append(
            lax.dot_general(
                left, weights, (((1,), (1,)), ((), ())), preferred_element_type=jnp.float32
            )
        )
    parts = []
    for both, (_, right, grad, atoms) in zip(products, pairs):
        basis = right.shape[0]
        density, weighted = both[:, :basis], both[:, basis:]
        terms = jnp.concatenate(
            [
                density * grad(0, c).astype(jnp.float32)
                - weighted * grad(1, c).astype(jnp.float32)
                for c in range(3)
            ],
            axis=1,
        )
        high = terms.astype(jnp.bfloat16)
        low = (terms - high.astype(jnp.float32)).astype(jnp.bfloat16)
        pick = (lax.broadcasted_iota(jnp.int32, (ATOMS, basis), 0) == atoms).astype(jnp.bfloat16)
        parts.append(
            lax.dot_general(
                jnp.concatenate((pick, pick), axis=1),
                jnp.concatenate((high, low), axis=0),
                (((1,), (0,)), ((), ())),
                preferred_element_type=jnp.float32,
            )
        )
    return parts


def sort_kernel(dims, first, second, meta, table):
    width_x, width_y, slots = dims
    tail = 12 * slots
    for k in range(4):
        table[tail + k] = 0
    table[tail + 4] = meta[1]
    table[tail + 5] = meta[0]

    def place(s, carry):
        g = second[s]
        gx, gy = g // (width_y + 2) - 1, g % (width_y + 2) - 1
        inside_x = jnp.logical_and(gx >= 0, gx < width_x)
        inside_y = jnp.logical_and(gy >= 0, gy < width_y)
        at_end = jnp.logical_or(gy == 0, gy == width_y - 1)
        row = (gx > 0).astype(jnp.int32)
        column = (gy > 0).astype(jnp.int32)
        rest = jnp.where(inside_y, 2 + row, 3)
        stage = jnp.where(
            inside_x, jnp.where(inside_y, 0, 1), jnp.where(at_end, 1, rest)
        )
        spot = jnp.where(
            inside_x,
            jnp.where(inside_y, gx * width_y + gy, column * width_x + gx),
            jnp.where(
                inside_y,
                jnp.where(at_end, 2 * width_x + 2 * row + column, gy - 1),
                width_y - 2 + 2 * column + row,
            ),
        )
        used = table[tail + stage]
        base = stage * 3 * slots + used
        table[base] = s
        table[base + slots] = first[s]
        table[base + 2 * slots] = spot
        table[tail + stage] = used + 1
        return carry

    lax.fori_loop(0, meta[0], place, 0)


def stage_body(
    dims, stage, right, table, coeffs, grads, occ, energy, atoms, acc, ready=lambda slot, done: done
):
    slots = dims[2]
    half_rows = grads[0].shape[2]
    number, half = table[12 * slots + stage], table[12 * slots + 4]
    offsets = [pl.multiple_of(part * half_rows, half_rows) for part in (half, 1 - half)]

    def visit(i, done):
        final = jnp.minimum(i * GROUP + GROUP - 1, number - 1)
        done = ready(table[stage * 3 * slots + final], done)
        pairs, targets = [], []
        for q in range(GROUP):
            entry = i * GROUP + q
            base = stage * 3 * slots + jnp.minimum(entry, number - 1)
            s, own, spot = table[base], table[base + slots], table[base + 2 * slots]
            left = jnp.concatenate(
                [coeffs[own, pl.ds(offset, half_rows), :] for offset in offsets], axis=0
            )

            def grad(kind, c, s=s):
                return jnp.concatenate(
                    (grads[2 * kind][s, c], grads[2 * kind + 1][s, c]), axis=0
                )

            pairs.append((left, right(spot), grad, atoms[pl.ds(own, 1), :]))
            targets.append((own, entry < number))
        for (own, live), part in zip(targets, pair_terms(pairs, occ[...], energy[...])):
            acc[own] += jnp.where(live, part, 0.0)
        return done

    return lax.fori_loop(0, (number + GROUP - 1) // GROUP, visit, 0)


def own_kernel(
    dims, table, coeffs, gh, gs, gh_far, gs_far, occ, energy, atoms, acc, gh2, gs2, sems
):
    slots = dims[2]
    chunks = (table[12 * slots + 5] + CHUNK - 1) // CHUNK

    def copies(k):
        part = pl.ds(pl.multiple_of(k * CHUNK, CHUNK), CHUNK)
        return [
            pltpu.make_async_copy(far.at[part], near.at[part], sems.at[k, n])
            for n, (far, near) in enumerate(((gh_far, gh2), (gs_far, gs2)))
        ]

    def start(k, carry):
        for copy in copies(k):
            copy.start()
        return carry

    def wait(k, carry):
        for copy in copies(k):
            copy.wait()
        return carry

    def ready(slot, done):
        need = jnp.maximum(slot // CHUNK + 1, done)
        lax.fori_loop(done, need, wait, 0)
        return need

    lax.fori_loop(0, chunks, start, 0)
    acc[...] = jnp.zeros_like(acc)
    done = stage_body(
        dims, 0, lambda spot: coeffs[spot], table, coeffs, (gh, gh2, gs, gs2), occ, energy, atoms,
        acc, ready,
    )
    lax.fori_loop(done, chunks, wait, 0)


def side_kernel(
    dims, table, coeffs, gh, gh2, gs, gs2, occ, energy, atoms, before, *rest
):
    rims, acc, cells, sems = rest[:-3], rest[-3], rest[-2], rest[-1]
    copies, start = [], 0
    for k, rim in enumerate(rims):
        size = rim.shape[0]
        copies.append(pltpu.make_async_copy(rim, cells.at[pl.ds(start, size)], sems.at[k]))
        start += size
    for copy in copies:
        copy.start()
    acc[...] = before[...]
    for copy in copies:
        copy.wait()
    stage_body(
        dims, 1, lambda spot: cells[spot], table, coeffs, (gh, gh2, gs, gs2), occ, energy, atoms, acc,
    )


def low_kernel(
    dims, table, coeffs, gh, gh2, gs, gs2, occ, energy, atoms, before, rim, acc
):
    acc[...] = before[...]
    stage_body(
        dims, 2, lambda spot: rim[spot], table, coeffs, (gh, gh2, gs, gs2), occ, energy, atoms, acc
    )


def last_kernel(
    dims, table, coeffs, gh, gh2, gs, gs2, occ, energy, atoms, before, *rest
):
    rims, out, acc = rest[:-2], rest[-2], rest[-1]
    acc[...] = before[...]

    def right(spot):
        start, cell = 0, None
        for rim in rims:
            size = rim.shape[0]
            here = rim[jnp.clip(spot - start, 0, size - 1)]
            cell = here if cell is None else jnp.where(spot >= start, here, cell)
            start += size
        return cell

    stage_body(
        dims, 3, right, table, coeffs, (gh, gh2, gs, gs2), occ, energy, atoms, acc
    )
    basis = atoms.shape[1]
    for c in range(3):
        out[c] = -2.0 * jnp.sum(acc[:, :, c * basis : (c + 1) * basis], axis=2)


def per_device(
    coeffs, occupation, energies, row_atom, pair_first, pair_second, pair_count, deriv_h, deriv_s
):
    width_x, width_y, basis, columns = coeffs.shape
    half_rows = row_atom.shape[2]
    local = width_x * width_y
    slots = pair_first.shape[2]
    dims = (width_x, width_y, slots)

    grad_h = deriv_h.reshape(slots, 3, half_rows, basis)
    grad_s = deriv_s.reshape(slots, 3, half_rows, basis)
    grad_h_far, grad_s_far = shift(grad_h, "orb", 1), shift(grad_s, "orb", 1)
    low_edge = shift(coeffs[width_x - 1, :: width_y - 1], "cx", 1)
    high_edge = shift(coeffs[0, :: width_y - 1], "cx", -1)
    low_mid = shift(coeffs[width_x - 1, 1 : width_y - 1], "cx", 1)
    low_side = shift(after(coeffs[:, width_y - 1], low_edge), "cy", 1)
    high_side = shift(after(coeffs[:, 0], high_edge), "cy", -1)
    high_mid = shift(coeffs[0, 1 : width_y - 1], "cx", -1)
    low_corner = shift(jnp.stack((low_edge[1], high_edge[1])), "cy", 1)
    high_corner = shift(jnp.stack((low_edge[0], high_edge[0])), "cy", -1)

    half = lax.axis_index("orb")
    atoms_own = row_atom.reshape(local, half_rows)
    atoms_all = lax.all_gather(atoms_own, "orb", axis=0)
    atoms = jnp.concatenate(
        (atoms_own, jnp.where(half == 0, atoms_all[1], atoms_all[0])), axis=1
    )

    flat = coeffs.reshape(local, basis, columns)
    first, second = pair_first.reshape(slots), pair_second.reshape(slots)
    meta = jnp.stack((pair_count.reshape(()), half.astype(jnp.int32)))
    occ, energy = occupation.reshape(1, columns), energies.reshape(1, columns)

    acc_shape = jax.ShapeDtypeStruct((local, ATOMS, 3 * basis), jnp.float32)
    params = pltpu.CompilerParams(vmem_limit_bytes=6 * 1024 * 1024)

    def cost(share):
        pairs = int(slots * share)
        return pl.CostEstimate(
            flops=pairs * basis * 2 * basis * columns * 2,
            bytes_accessed=pairs * 2 * (2 * basis * columns + 6 * basis * basis),
            transcendentals=0,
        )

    table = pl.pallas_call(
        functools.partial(sort_kernel, dims),
        out_shape=jax.ShapeDtypeStruct((12 * slots + 8,), jnp.int32),
        in_specs=[SMEM] * 3,
        out_specs=SMEM,
        compiler_params=pltpu.CompilerParams(vmem_limit_bytes=1024 * 1024),
    )(first, second, meta)
    acc, grad_h2, grad_s2 = pl.pallas_call(
        functools.partial(own_kernel, dims),
        out_shape=(
            acc_shape,
            jax.ShapeDtypeStruct(grad_h.shape, grad_h.dtype),
            jax.ShapeDtypeStruct(grad_s.shape, grad_s.dtype),
        ),
        in_specs=[SMEM] + [VMEM] * 3 + [ANY] * 2 + [VMEM] * 3,
        out_specs=(VMEM, VMEM, VMEM),
        scratch_shapes=[pltpu.SemaphoreType.DMA((slots // CHUNK, 2))],
        compiler_params=params,
        cost_estimate=cost(0.75),
    )(table, flat, grad_h, grad_s, grad_h_far, grad_s_far, occ, energy, atoms)
    common = (table, flat, grad_h, grad_h2, grad_s, grad_s2, occ, energy, atoms)
    common_specs = [SMEM] + [VMEM] * 8
    rims = (low_side, high_side, low_edge, high_edge)
    acc = pl.pallas_call(
        functools.partial(side_kernel, dims),
        out_shape=acc_shape,
        in_specs=common_specs + [VMEM] * (1 + len(rims)),
        out_specs=VMEM,
        scratch_shapes=[
            pltpu.VMEM((sum(rim.shape[0] for rim in rims), basis, columns), jnp.bfloat16),
            pltpu.SemaphoreType.DMA((len(rims),)),
        ],
        compiler_params=params,
        cost_estimate=cost(0.15),
    )(*common, acc, *rims)
    acc = pl.pallas_call(
        functools.partial(low_kernel, dims),
        out_shape=acc_shape,
        in_specs=common_specs + [VMEM] * 2,
        out_specs=VMEM,
        compiler_params=params,
        cost_estimate=cost(0.1),
    )(*common, acc, low_mid)
    out = pl.pallas_call(
        functools.partial(last_kernel, dims),
        out_shape=jax.ShapeDtypeStruct((3, local, ATOMS), jnp.float32),
        in_specs=common_specs + [VMEM] * 4,
        out_specs=VMEM,
        scratch_shapes=[pltpu.VMEM(acc_shape.shape, jnp.float32)],
        compiler_params=params,
        cost_estimate=cost(0.1),
    )(*common, acc, high_mid, low_corner, high_corner)
    total = out + shift(out, "orb", 1)
    return total.reshape(3, width_x, width_y, ATOMS)


def solution(mesh):
    return jax.shard_map(
        per_device,
        mesh=mesh,
        in_specs=(
            P("cx", "cy", None, "orb"),
            P("orb"),
            P("orb"),
            P("cx", "cy", "orb"),
            P("cx", "cy", None),
            P("cx", "cy", None),
            P("cx", "cy"),
            P("cx", "cy", None, None, "orb", None),
            P("cx", "cy", None, None, "orb", None),
        ),
        out_specs=P(None, "cx", "cy", None),
        check_vma=False,
    )
```

```python
import functools

import jax
import jax.numpy as jnp
import numpy as np
from jax import lax
from jax.experimental import pallas as pl
from jax.experimental.pallas import tpu as pltpu
from jax.sharding import PartitionSpec as P

ATOMS = 8
GROUP = 4
SHIFT_BITS = 16
SHIFT = 1 << SHIFT_BITS
OWN_GROUP = 6
CHUNK = 8
ANY = pl.BlockSpec(memory_space=pl.ANY)
SMEM = pl.BlockSpec(memory_space=pltpu.SMEM)
VMEM = pl.BlockSpec(memory_space=pltpu.VMEM)


def shift(cells, axis, step):
    count = lax.axis_size(axis)
    return lax.ppermute(cells, axis, [(i, (i + step) % count) for i in range(count)])


def after(cells, *others):
    return lax.optimization_barrier((cells, *others))[0]


def pair_terms(pairs, occ, energy):
    products = []
    for left, right, _, _ in pairs:
        scaled = right.astype(jnp.float32) * occ
        weights = jnp.concatenate(
            (scaled.astype(jnp.bfloat16), (scaled * energy).astype(jnp.bfloat16)), axis=0
        )
        products.append(
            lax.dot_general(
                left, weights, (((1,), (1,)), ((), ())), preferred_element_type=jnp.float32
            )
        )
    parts = []
    for both, (_, right, grad, atoms) in zip(products, pairs):
        basis = right.shape[0]
        density, weighted = both[:, :basis], both[:, basis:]
        terms = jnp.concatenate(
            [
                density * grad(0, c).astype(jnp.float32)
                - weighted * grad(1, c).astype(jnp.float32)
                for c in range(3)
            ],
            axis=1,
        )
        high = terms.astype(jnp.bfloat16)
        low = (terms - high.astype(jnp.float32)).astype(jnp.bfloat16)
        pick = (lax.broadcasted_iota(jnp.int32, (ATOMS, basis), 0) == atoms).astype(jnp.bfloat16)
        parts.append(
            lax.dot_general(
                jnp.concatenate((pick, pick), axis=1),
                jnp.concatenate((high, low), axis=0),
                (((1,), (0,)), ((), ())),
                preferred_element_type=jnp.float32,
            )
        )
    return parts


def places_of(dims):
    width_x, width_y, _ = dims
    codes = []
    for gx in range(-1, width_x + 1):
        for gy in range(-1, width_y + 1):
            row, column = int(gx >= width_x), int(gy > 0)
            inside_x, inside_y = 0 <= gx < width_x, 0 <= gy < width_y
            if inside_x:
                code = (0, gx * width_y + gy) if inside_y else (1, column * width_x + gx)
            elif not inside_y:
                code = 3, width_y - 2 + 2 * int(gy >= width_y) + row
            elif gy in (0, width_y - 1):
                code = 1, 2 * width_x + 2 * row + column
            else:
                code = 2 + row, gy - 1
            codes.append(code[0] * SHIFT + code[1])
    return np.array(codes, np.int32)


def sort_kernel(dims, first, second, meta, codes, atoms, coeffs, gs, table, atoms_out):
    atoms_out[...] = atoms[...]
    slots = dims[2]
    tail = 12 * slots
    for k in range(4):
        table[tail + k] = 0
    table[tail + 4] = meta[1]
    table[tail + 5] = meta[0]

    def place(s, carry):
        code = codes[second[s]]
        stage = lax.shift_right_logical(code, SHIFT_BITS)
        used = table[tail + stage]
        base = stage * 3 * slots + used
        table[base] = s
        table[base + slots] = first[s]
        table[base + 2 * slots] = lax.bitwise_and(code, SHIFT - 1)
        table[tail + stage] = used + 1
        return carry

    lax.fori_loop(0, meta[0], place, 0)


def stage_body(
    dims, stage, right, table, coeffs, grads, occ, energy, atoms, acc, group=GROUP,
    ready=lambda slot, done: done,
):
    slots = dims[2]
    half_rows = grads[0].shape[2]
    number, half = table[12 * slots + stage], table[12 * slots + 4]
    offsets = [pl.multiple_of(part * half_rows, half_rows) for part in (half, 1 - half)]

    def visit(i, done):
        final = jnp.minimum(i * group + group - 1, number - 1)
        done = ready(table[stage * 3 * slots + final], done)
        pairs, targets = [], []
        for q in range(group):
            entry = i * group + q
            base = stage * 3 * slots + jnp.minimum(entry, number - 1)
            s, own, spot = table[base], table[base + slots], table[base + 2 * slots]
            left = jnp.concatenate(
                [coeffs[own, pl.ds(offset, half_rows), :] for offset in offsets], axis=0
            )

            def grad(kind, c, s=s):
                return jnp.concatenate(
                    (grads[2 * kind][s, c], grads[2 * kind + 1][s, c]), axis=0
                )

            pairs.append((left, right(spot), grad, atoms[pl.ds(own, 1), :]))
            targets.append((own, entry < number))
        for (own, live), part in zip(targets, pair_terms(pairs, occ[...], energy[...])):
            acc[own] += jnp.where(live, part, 0.0)
        return done

    return lax.fori_loop(0, (number + group - 1) // group, visit, 0)


def own_kernel(
    dims, table, coeffs, gh, gs, gh_far, gs_far, occ, energy, atoms, acc, gh2, gs2, sems
):
    slots = dims[2]
    chunks = (table[12 * slots + 5] + CHUNK - 1) // CHUNK

    def copies(k):
        part = pl.ds(pl.multiple_of(k * CHUNK, CHUNK), CHUNK)
        return [
            pltpu.make_async_copy(far.at[part], near.at[part], sems.at[k, n])
            for n, (far, near) in enumerate(((gh_far, gh2), (gs_far, gs2)))
        ]

    def start(k, carry):
        for copy in copies(k):
            copy.start()
        return carry

    def wait(k, carry):
        for copy in copies(k):
            copy.wait()
        return carry

    def ready(slot, done):
        need = jnp.maximum(slot // CHUNK + 1, done)
        lax.fori_loop(done, need, wait, 0)
        return need

    lax.fori_loop(0, chunks, start, 0)
    acc[...] = jnp.zeros_like(acc)
    done = stage_body(
        dims, 0, lambda spot: coeffs[spot], table, coeffs, (gh, gh2, gs, gs2), occ, energy, atoms,
        acc, OWN_GROUP, ready,
    )
    lax.fori_loop(done, chunks, wait, 0)


def side_kernel(
    dims, table, coeffs, gh, gh2, gs, gs2, occ, energy, atoms, before, *rest
):
    rims, acc, cells, sems = rest[:-3], rest[-3], rest[-2], rest[-1]
    copies, start = [], 0
    for k, rim in enumerate(rims):
        size = rim.shape[0]
        copies.append(pltpu.make_async_copy(rim, cells.at[pl.ds(start, size)], sems.at[k]))
        start += size
    for copy in copies:
        copy.start()
    acc[...] = before[...]
    for copy in copies:
        copy.wait()
    stage_body(
        dims, 1, lambda spot: cells[spot], table, coeffs, (gh, gh2, gs, gs2), occ, energy, atoms, acc,
    )


def low_kernel(
    dims, table, coeffs, gh, gh2, gs, gs2, occ, energy, atoms, before, rim, acc
):
    acc[...] = before[...]
    stage_body(
        dims, 2, lambda spot: rim[spot], table, coeffs, (gh, gh2, gs, gs2), occ, energy, atoms, acc
    )


def last_kernel(
    dims, table, coeffs, gh, gh2, gs, gs2, occ, energy, atoms, before, *rest
):
    rims, out, acc = rest[:-2], rest[-2], rest[-1]
    acc[...] = before[...]

    def right(spot):
        start, cell = 0, None
        for rim in rims:
            size = rim.shape[0]
            here = rim[jnp.clip(spot - start, 0, size - 1)]
            cell = here if cell is None else jnp.where(spot >= start, here, cell)
            start += size
        return cell

    stage_body(
        dims, 3, right, table, coeffs, (gh, gh2, gs, gs2), occ, energy, atoms, acc
    )
    basis = atoms.shape[1]
    for c in range(3):
        out[c] = -2.0 * jnp.sum(acc[:, :, c * basis : (c + 1) * basis], axis=2)


def per_device(
    coeffs, occupation, energies, row_atom, pair_first, pair_second, pair_count, deriv_h, deriv_s
):
    width_x, width_y, basis, columns = coeffs.shape
    half_rows = row_atom.shape[2]
    local = width_x * width_y
    slots = pair_first.shape[2]
    dims = (width_x, width_y, slots)

    grad_h = deriv_h.reshape(slots, 3, half_rows, basis)
    grad_s = deriv_s.reshape(slots, 3, half_rows, basis)
    grad_h_far, grad_s_far = shift(grad_h, "orb", 1), shift(grad_s, "orb", 1)
    low_edge = shift(coeffs[width_x - 1, :: width_y - 1], "cx", 1)
    high_edge = shift(coeffs[0, :: width_y - 1], "cx", -1)
    low_mid = shift(coeffs[width_x - 1, 1 : width_y - 1], "cx", 1)
    low_side = shift(after(coeffs[:, width_y - 1], low_edge), "cy", 1)
    high_side = shift(after(coeffs[:, 0], grad_h_far), "cy", -1)
    high_mid = shift(after(coeffs[0, 1 : width_y - 1], high_edge), "cx", -1)
    low_corner = shift(jnp.stack((low_edge[1], high_edge[1])), "cy", 1)
    high_corner = shift(jnp.stack((low_edge[0], high_edge[0])), "cy", -1)

    half = lax.axis_index("orb")
    atoms_own = row_atom.reshape(local, half_rows)
    atoms_all = lax.all_gather(atoms_own, "orb", axis=0)
    atoms = jnp.concatenate(
        (atoms_own, jnp.where(half == 0, atoms_all[1], atoms_all[0])), axis=1
    )

    flat = coeffs.reshape(local, basis, columns)
    first, second = pair_first.reshape(slots), pair_second.reshape(slots)
    meta = jnp.stack((pair_count.reshape(()), half.astype(jnp.int32)))
    occ, energy = occupation.reshape(1, columns), energies.reshape(1, columns)

    acc_shape = jax.ShapeDtypeStruct((local, ATOMS, 3 * basis), jnp.float32)
    params = pltpu.CompilerParams(vmem_limit_bytes=6 * 1024 * 1024)

    def cost(share):
        pairs = int(slots * share)
        return pl.CostEstimate(
            flops=pairs * basis * 2 * basis * columns * 2,
            bytes_accessed=pairs * 2 * (2 * basis * columns + 6 * basis * basis),
            transcendentals=0,
        )

    table, atoms = pl.pallas_call(
        functools.partial(sort_kernel, dims),
        out_shape=(
            jax.ShapeDtypeStruct((12 * slots + 8,), jnp.int32),
            jax.ShapeDtypeStruct(atoms.shape, atoms.dtype),
        ),
        in_specs=[SMEM] * 4 + [VMEM] * 3,
        out_specs=(SMEM, VMEM),
        compiler_params=pltpu.CompilerParams(vmem_limit_bytes=1024 * 1024),
    )(first, second, meta, places_of(dims), atoms, flat, grad_s)
    acc, grad_h2, grad_s2 = pl.pallas_call(
        functools.partial(own_kernel, dims),
        out_shape=(
            acc_shape,
            jax.ShapeDtypeStruct(grad_h.shape, grad_h.dtype),
            jax.ShapeDtypeStruct(grad_s.shape, grad_s.dtype),
        ),
        in_specs=[SMEM] + [VMEM] * 3 + [ANY] * 2 + [VMEM] * 3,
        out_specs=(VMEM, VMEM, VMEM),
        scratch_shapes=[pltpu.SemaphoreType.DMA((slots // CHUNK, 2))],
        compiler_params=params,
        cost_estimate=cost(0.75),
    )(table, flat, grad_h, grad_s, grad_h_far, grad_s_far, occ, energy, atoms)
    common = (table, flat, grad_h, grad_h2, grad_s, grad_s2, occ, energy, atoms)
    common_specs = [SMEM] + [VMEM] * 8
    rims = (low_side, high_side, low_edge, high_edge)
    acc = pl.pallas_call(
        functools.partial(side_kernel, dims),
        out_shape=acc_shape,
        in_specs=common_specs + [VMEM] * (1 + len(rims)),
        out_specs=VMEM,
        scratch_shapes=[
            pltpu.VMEM((sum(rim.shape[0] for rim in rims), basis, columns), jnp.bfloat16),
            pltpu.SemaphoreType.DMA((len(rims),)),
        ],
        compiler_params=params,
        cost_estimate=cost(0.15),
    )(*common, acc, *rims)
    acc = pl.pallas_call(
        functools.partial(low_kernel, dims),
        out_shape=acc_shape,
        in_specs=common_specs + [VMEM] * 2,
        out_specs=VMEM,
        compiler_params=params,
        cost_estimate=cost(0.1),
    )(*common, acc, low_mid)
    out = pl.pallas_call(
        functools.partial(last_kernel, dims),
        out_shape=jax.ShapeDtypeStruct((3, local, ATOMS), jnp.float32),
        in_specs=common_specs + [VMEM] * 4,
        out_specs=VMEM,
        scratch_shapes=[pltpu.VMEM(acc_shape.shape, jnp.float32)],
        compiler_params=params,
        cost_estimate=cost(0.1),
    )(*common, acc, high_mid, low_corner, high_corner)
    total = out + shift(out, "orb", 1)
    return total.reshape(3, width_x, width_y, ATOMS)


def solution(mesh):
    return jax.shard_map(
        per_device,
        mesh=mesh,
        in_specs=(
            P("cx", "cy", None, "orb"),
            P("orb"),
            P("orb"),
            P("cx", "cy", "orb"),
            P("cx", "cy", None),
            P("cx", "cy", None),
            P("cx", "cy"),
            P("cx", "cy", None, None, "orb", None),
            P("cx", "cy", None, None, "orb", None),
        ),
        out_specs=P(None, "cx", "cy", None),
        check_vma=False,
    )
```

```python
import functools

import jax
import jax.numpy as jnp
import numpy as np
from jax import lax
from jax.experimental import pallas as pl
from jax.experimental.pallas import tpu as pltpu
from jax.sharding import PartitionSpec as P

ATOMS = 8
GROUP = 4
SHIFT_BITS = 16
SHIFT = 1 << SHIFT_BITS
OWN_GROUP = 6
CHUNK = 8
ANY = pl.BlockSpec(memory_space=pl.ANY)
SMEM = pl.BlockSpec(memory_space=pltpu.SMEM)
VMEM = pl.BlockSpec(memory_space=pltpu.VMEM)


def shift(cells, axis, step):
    count = lax.axis_size(axis)
    return lax.ppermute(cells, axis, [(i, (i + step) % count) for i in range(count)])


def after(cells, *others):
    return lax.optimization_barrier((cells, *others))[0]


def pair_terms(pairs, occ, energy):
    products = []
    for left, right, _, _ in pairs:
        scaled = right.astype(jnp.float32) * occ
        weights = jnp.concatenate(
            (scaled.astype(jnp.bfloat16), (scaled * energy).astype(jnp.bfloat16)), axis=0
        )
        products.append(
            lax.dot_general(
                left, weights, (((1,), (1,)), ((), ())), preferred_element_type=jnp.float32
            )
        )
    parts = []
    for both, (_, right, grad, atoms) in zip(products, pairs):
        basis = right.shape[0]
        density, weighted = both[:, :basis], both[:, basis:]
        terms = jnp.concatenate(
            [
                density * grad(0, c).astype(jnp.float32)
                - weighted * grad(1, c).astype(jnp.float32)
                for c in range(3)
            ],
            axis=1,
        )
        high = terms.astype(jnp.bfloat16)
        low = (terms - high.astype(jnp.float32)).astype(jnp.bfloat16)
        pick = (lax.broadcasted_iota(jnp.int32, (ATOMS, basis), 0) == atoms).astype(jnp.bfloat16)
        parts.append(
            lax.dot_general(
                jnp.concatenate((pick, pick), axis=1),
                jnp.concatenate((high, low), axis=0),
                (((1,), (0,)), ((), ())),
                preferred_element_type=jnp.float32,
            )
        )
    return parts


def places_of(dims):
    width_x, width_y, _ = dims
    codes = []
    for gx in range(-1, width_x + 1):
        for gy in range(-1, width_y + 1):
            row, column = int(gx >= width_x), int(gy > 0)
            inside_x, inside_y = 0 <= gx < width_x, 0 <= gy < width_y
            if inside_x:
                code = (0, gx * width_y + gy) if inside_y else (1, column * width_x + gx)
            elif not inside_y:
                code = 3, width_y - 2 + 2 * int(gy >= width_y) + row
            elif gy in (0, width_y - 1):
                code = 1, 2 * width_x + 2 * row + column
            else:
                code = 2 + row, gy - 1
            codes.append(code[0] * SHIFT + code[1])
    return np.array(codes, np.int32)


def sort_kernel(dims, first, second, meta, codes, atoms, coeffs, gs, table, atoms_out):
    atoms_out[...] = atoms[...]
    slots = dims[2]
    tail = 12 * slots
    for k in range(4):
        table[tail + k] = 0
    table[tail + 4] = meta[1]
    table[tail + 5] = meta[0]

    def place(s, carry):
        code = codes[second[s]]
        stage = lax.shift_right_logical(code, SHIFT_BITS)
        used = table[tail + stage]
        base = stage * 3 * slots + used
        table[base] = s
        table[base + slots] = first[s]
        table[base + 2 * slots] = lax.bitwise_and(code, SHIFT - 1)
        table[tail + stage] = used + 1
        return carry

    lax.fori_loop(0, meta[0], place, 0)


def stage_body(
    dims, stage, right, table, coeffs, grads, occ, energy, atoms, acc, group=GROUP,
    ready=lambda slot, done: done,
):
    slots = dims[2]
    half_rows = grads[0].shape[2]
    number, half = table[12 * slots + stage], table[12 * slots + 4]
    offsets = [pl.multiple_of(part * half_rows, half_rows) for part in (half, 1 - half)]

    def visit(i, done):
        final = jnp.minimum(i * group + group - 1, number - 1)
        done = ready(table[stage * 3 * slots + final], done)
        pairs, targets = [], []
        for q in range(group):
            entry = i * group + q
            base = stage * 3 * slots + jnp.minimum(entry, number - 1)
            s, own, spot = table[base], table[base + slots], table[base + 2 * slots]
            left = jnp.concatenate(
                [coeffs[own, pl.ds(offset, half_rows), :] for offset in offsets], axis=0
            )

            def grad(kind, c, s=s):
                return jnp.concatenate(
                    (grads[2 * kind][s, c], grads[2 * kind + 1][s, c]), axis=0
                )

            pairs.append((left, right(spot), grad, atoms[pl.ds(own, 1), :]))
            targets.append((own, entry < number))
        for (own, live), part in zip(targets, pair_terms(pairs, occ[...], energy[...])):
            acc[own] += jnp.where(live, part, 0.0)
        return done

    return lax.fori_loop(0, (number + group - 1) // group, visit, 0)


def own_kernel(
    dims, table, coeffs, gh, gs, gh_far, gs_far, occ, energy, atoms, acc, gh2, gs2, sems
):
    slots = dims[2]
    chunks = (table[12 * slots + 5] + CHUNK - 1) // CHUNK

    def copies(k):
        part = pl.ds(pl.multiple_of(k * CHUNK, CHUNK), CHUNK)
        return [
            pltpu.make_async_copy(far.at[part], near.at[part], sems.at[k, n])
            for n, (far, near) in enumerate(((gh_far, gh2), (gs_far, gs2)))
        ]

    def start(k, carry):
        for copy in copies(k):
            copy.start()
        return carry

    def wait(k, carry):
        for copy in copies(k):
            copy.wait()
        return carry

    def ready(slot, done):
        need = jnp.maximum(slot // CHUNK + 1, done)
        lax.fori_loop(done, need, wait, 0)
        return need

    lax.fori_loop(0, chunks, start, 0)
    acc[...] = jnp.zeros_like(acc)
    done = stage_body(
        dims, 0, lambda spot: coeffs[spot], table, coeffs, (gh, gh2, gs, gs2), occ, energy, atoms,
        acc, OWN_GROUP, ready,
    )
    lax.fori_loop(done, chunks, wait, 0)


def side_kernel(
    dims, table, coeffs, gh, gh2, gs, gs2, occ, energy, atoms, before, *rest
):
    rims, acc, cells, sems = rest[:-3], rest[-3], rest[-2], rest[-1]
    copies, start = [], 0
    for k, rim in enumerate(rims):
        size = rim.shape[0]
        copies.append(pltpu.make_async_copy(rim, cells.at[pl.ds(start, size)], sems.at[k]))
        start += size
    for copy in copies:
        copy.start()
    acc[...] = before[...]
    for copy in copies:
        copy.wait()
    stage_body(
        dims, 1, lambda spot: cells[spot], table, coeffs, (gh, gh2, gs, gs2), occ, energy, atoms, acc,
    )


def low_kernel(
    dims, table, coeffs, gh, gh2, gs, gs2, occ, energy, atoms, before, rim, acc
):
    acc[...] = before[...]
    stage_body(
        dims, 2, lambda spot: rim[spot], table, coeffs, (gh, gh2, gs, gs2), occ, energy, atoms, acc
    )


def last_kernel(
    dims, table, coeffs, gh, gh2, gs, gs2, occ, energy, atoms, before, *rest
):
    rims, out, acc = rest[:-2], rest[-2], rest[-1]
    acc[...] = before[...]

    def right(spot):
        start, cell = 0, None
        for rim in rims:
            size = rim.shape[0]
            here = rim[jnp.clip(spot - start, 0, size - 1)]
            cell = here if cell is None else jnp.where(spot >= start, here, cell)
            start += size
        return cell

    stage_body(
        dims, 3, right, table, coeffs, (gh, gh2, gs, gs2), occ, energy, atoms, acc
    )
    basis = atoms.shape[1]
    for c in range(3):
        out[c] = -2.0 * jnp.sum(acc[:, :, c * basis : (c + 1) * basis], axis=2)


def per_device(
    coeffs, occupation, energies, row_atom, pair_first, pair_second, pair_count, deriv_h, deriv_s
):
    width_x, width_y, basis, columns = coeffs.shape
    half_rows = row_atom.shape[2]
    local = width_x * width_y
    slots = pair_first.shape[2]
    dims = (width_x, width_y, slots)

    grad_h = deriv_h.reshape(slots, 3, half_rows, basis)
    grad_s = deriv_s.reshape(slots, 3, half_rows, basis)
    grad_h_far, grad_s_far = shift(grad_h, "orb", 1), shift(grad_s, "orb", 1)
    low_edge = shift(coeffs[width_x - 1, :: width_y - 1], "cx", 1)
    high_edge = shift(coeffs[0, :: width_y - 1], "cx", -1)
    low_mid = shift(coeffs[width_x - 1, 1 : width_y - 1], "cx", 1)
    low_side = shift(after(coeffs[:, width_y - 1], low_edge), "cy", 1)
    high_side = shift(after(coeffs[:, 0], high_edge), "cy", -1)
    high_mid = shift(after(coeffs[0, 1 : width_y - 1], high_edge, low_edge), "cx", -1)
    low_corner = shift(jnp.stack((low_edge[1], high_edge[1])), "cy", 1)
    high_corner = shift(jnp.stack((low_edge[0], high_edge[0])), "cy", -1)

    half = lax.axis_index("orb")
    atoms_own = row_atom.reshape(local, half_rows)
    atoms_all = lax.all_gather(atoms_own, "orb", axis=0)
    atoms = jnp.concatenate(
        (atoms_own, jnp.where(half == 0, atoms_all[1], atoms_all[0])), axis=1
    )

    flat = coeffs.reshape(local, basis, columns)
    first, second = pair_first.reshape(slots), pair_second.reshape(slots)
    meta = jnp.stack((pair_count.reshape(()), half.astype(jnp.int32)))
    occ, energy = occupation.reshape(1, columns), energies.reshape(1, columns)

    acc_shape = jax.ShapeDtypeStruct((local, ATOMS, 3 * basis), jnp.float32)
    params = pltpu.CompilerParams(vmem_limit_bytes=6 * 1024 * 1024)

    def cost(share):
        pairs = int(slots * share)
        return pl.CostEstimate(
            flops=pairs * basis * 2 * basis * columns * 2,
            bytes_accessed=pairs * 2 * (2 * basis * columns + 6 * basis * basis),
            transcendentals=0,
        )

    table, atoms = pl.pallas_call(
        functools.partial(sort_kernel, dims),
        out_shape=(
            jax.ShapeDtypeStruct((12 * slots + 8,), jnp.int32),
            jax.ShapeDtypeStruct(atoms.shape, atoms.dtype),
        ),
        in_specs=[SMEM] * 4 + [VMEM] * 3,
        out_specs=(SMEM, VMEM),
        compiler_params=pltpu.CompilerParams(vmem_limit_bytes=12 * 1024 * 1024),
    )(first, second, meta, places_of(dims), atoms, flat, grad_s)
    acc, grad_h2, grad_s2 = pl.pallas_call(
        functools.partial(own_kernel, dims),
        out_shape=(
            acc_shape,
            jax.ShapeDtypeStruct(grad_h.shape, grad_h.dtype),
            jax.ShapeDtypeStruct(grad_s.shape, grad_s.dtype),
        ),
        in_specs=[SMEM] + [VMEM] * 3 + [ANY] * 2 + [VMEM] * 3,
        out_specs=(VMEM, VMEM, VMEM),
        scratch_shapes=[pltpu.SemaphoreType.DMA((slots // CHUNK, 2))],
        compiler_params=params,
        cost_estimate=cost(0.75),
    )(table, flat, grad_h, grad_s, grad_h_far, grad_s_far, occ, energy, atoms)
    common = (table, flat, grad_h, grad_h2, grad_s, grad_s2, occ, energy, atoms)
    common_specs = [SMEM] + [VMEM] * 8
    rims = (low_side, high_side, low_edge, high_edge)
    acc = pl.pallas_call(
        functools.partial(side_kernel, dims),
        out_shape=acc_shape,
        in_specs=common_specs + [VMEM] * (1 + len(rims)),
        out_specs=VMEM,
        scratch_shapes=[
            pltpu.VMEM((sum(rim.shape[0] for rim in rims), basis, columns), jnp.bfloat16),
            pltpu.SemaphoreType.DMA((len(rims),)),
        ],
        compiler_params=params,
        cost_estimate=cost(0.15),
    )(*common, acc, *rims)
    acc = pl.pallas_call(
        functools.partial(low_kernel, dims),
        out_shape=acc_shape,
        in_specs=common_specs + [VMEM] * 2,
        out_specs=VMEM,
        compiler_params=params,
        cost_estimate=cost(0.1),
    )(*common, acc, low_mid)
    out = pl.pallas_call(
        functools.partial(last_kernel, dims),
        out_shape=jax.ShapeDtypeStruct((3, local, ATOMS), jnp.float32),
        in_specs=common_specs + [VMEM] * 4,
        out_specs=VMEM,
        scratch_shapes=[pltpu.VMEM(acc_shape.shape, jnp.float32)],
        compiler_params=params,
        cost_estimate=cost(0.1),
    )(*common, acc, high_mid, low_corner, high_corner)
    total = out + shift(out, "orb", 1)
    return total.reshape(3, width_x, width_y, ATOMS)


def solution(mesh):
    return jax.shard_map(
        per_device,
        mesh=mesh,
        in_specs=(
            P("cx", "cy", None, "orb"),
            P("orb"),
            P("orb"),
            P("cx", "cy", "orb"),
            P("cx", "cy", None),
            P("cx", "cy", None),
            P("cx", "cy"),
            P("cx", "cy", None, None, "orb", None),
            P("cx", "cy", None, None, "orb", None),
        ),
        out_specs=P(None, "cx", "cy", None),
        check_vma=False,
    )
```

```python
import functools

import jax
import jax.numpy as jnp
import numpy as np
from jax import lax
from jax.experimental import pallas as pl
from jax.experimental.pallas import tpu as pltpu
from jax.sharding import PartitionSpec as P

ATOMS = 8
GROUP = 4
SHIFT_BITS = 16
SHIFT = 1 << SHIFT_BITS
OWN_GROUP = 6
CHUNK = 8
ANY = pl.BlockSpec(memory_space=pl.ANY)
SMEM = pl.BlockSpec(memory_space=pltpu.SMEM)
VMEM = pl.BlockSpec(memory_space=pltpu.VMEM)


def shift(cells, axis, step):
    count = lax.axis_size(axis)
    return lax.ppermute(cells, axis, [(i, (i + step) % count) for i in range(count)])


def after(cells, *others):
    return lax.optimization_barrier((cells, *others))[0]


def pair_terms(pairs, occ, energy):
    products = []
    for left, right, _, _ in pairs:
        scaled = right.astype(jnp.float32) * occ
        weights = jnp.concatenate(
            (scaled.astype(jnp.bfloat16), (scaled * energy).astype(jnp.bfloat16)), axis=0
        )
        products.append(
            lax.dot_general(
                left, weights, (((1,), (1,)), ((), ())), preferred_element_type=jnp.float32
            )
        )
    parts = []
    for both, (_, right, grad, atoms) in zip(products, pairs):
        basis = right.shape[0]
        density, weighted = both[:, :basis], both[:, basis:]
        terms = jnp.concatenate(
            [
                density * grad(0, c).astype(jnp.float32)
                - weighted * grad(1, c).astype(jnp.float32)
                for c in range(3)
            ],
            axis=1,
        )
        high = terms.astype(jnp.bfloat16)
        low = (terms - high.astype(jnp.float32)).astype(jnp.bfloat16)
        pick = (lax.broadcasted_iota(jnp.int32, (ATOMS, basis), 0) == atoms).astype(jnp.bfloat16)
        parts.append(
            lax.dot_general(
                jnp.concatenate((pick, pick), axis=1),
                jnp.concatenate((high, low), axis=0),
                (((1,), (0,)), ((), ())),
                preferred_element_type=jnp.float32,
            )
        )
    return parts


def places_of(dims):
    width_x, width_y, _ = dims
    codes = []
    for gx in range(-1, width_x + 1):
        for gy in range(-1, width_y + 1):
            row, column = int(gx >= width_x), int(gy > 0)
            inside_x, inside_y = 0 <= gx < width_x, 0 <= gy < width_y
            if inside_x:
                code = (0, gx * width_y + gy) if inside_y else (1, column * width_x + gx)
            elif not inside_y:
                code = 3, width_y - 2 + 2 * int(gy >= width_y) + row
            elif gy in (0, width_y - 1):
                code = 1, 2 * width_x + 2 * row + column
            else:
                code = 2 + row, gy - 1
            codes.append(code[0] * SHIFT + code[1])
    return np.array(codes, np.int32)


def sort_kernel(dims, first, second, meta, codes, atoms, coeffs, gs, table, atoms_out):
    atoms_out[...] = atoms[...]
    slots = dims[2]
    tail = 12 * slots
    for k in range(4):
        table[tail + k] = 0
    table[tail + 4] = meta[1]
    table[tail + 5] = meta[0]

    def place(s, carry):
        code = codes[second[s]]
        stage = lax.shift_right_logical(code, SHIFT_BITS)
        used = table[tail + stage]
        base = stage * 3 * slots + used
        table[base] = s
        table[base + slots] = first[s]
        table[base + 2 * slots] = lax.bitwise_and(code, SHIFT - 1)
        table[tail + stage] = used + 1
        return carry

    lax.fori_loop(0, meta[0], place, 0)


def stage_body(
    dims, stage, right, table, coeffs, grads, occ, energy, atoms, acc, group=GROUP,
    ready=lambda slot, done: done,
):
    slots = dims[2]
    half_rows = grads[0].shape[2]
    number, half = table[12 * slots + stage], table[12 * slots + 4]
    offsets = [pl.multiple_of(part * half_rows, half_rows) for part in (half, 1 - half)]

    def visit(i, done):
        final = jnp.minimum(i * group + group - 1, number - 1)
        done = ready(table[stage * 3 * slots + final], done)
        pairs, targets = [], []
        for q in range(group):
            entry = i * group + q
            base = stage * 3 * slots + jnp.minimum(entry, number - 1)
            s, own, spot = table[base], table[base + slots], table[base + 2 * slots]
            left = jnp.concatenate(
                [coeffs[own, pl.ds(offset, half_rows), :] for offset in offsets], axis=0
            )

            def grad(kind, c, s=s):
                return jnp.concatenate(
                    (grads[2 * kind][s, c], grads[2 * kind + 1][s, c]), axis=0
                )

            pairs.append((left, right(spot), grad, atoms[pl.ds(own, 1), :]))
            targets.append((own, entry < number))
        for (own, live), part in zip(targets, pair_terms(pairs, occ[...], energy[...])):
            acc[own] += jnp.where(live, part, 0.0)
        return done

    return lax.fori_loop(0, (number + group - 1) // group, visit, 0)


def own_kernel(
    dims, table, coeffs, gh, gs, gh_far, gs_far, occ, energy, atoms, acc, gh2, gs2, sems
):
    slots = dims[2]
    chunks = (table[12 * slots + 5] + CHUNK - 1) // CHUNK

    def copies(k):
        part = pl.ds(pl.multiple_of(k * CHUNK, CHUNK), CHUNK)
        return [
            pltpu.make_async_copy(far.at[part], near.at[part], sems.at[k, n])
            for n, (far, near) in enumerate(((gh_far, gh2), (gs_far, gs2)))
        ]

    def start(k, carry):
        for copy in copies(k):
            copy.start()
        return carry

    def wait(k, carry):
        for copy in copies(k):
            copy.wait()
        return carry

    def ready(slot, done):
        need = jnp.maximum(slot // CHUNK + 1, done)
        lax.fori_loop(done, need, wait, 0)
        return need

    lax.fori_loop(0, chunks, start, 0)
    acc[...] = jnp.zeros_like(acc)
    done = stage_body(
        dims, 0, lambda spot: coeffs[spot], table, coeffs, (gh, gh2, gs, gs2), occ, energy, atoms,
        acc, OWN_GROUP, ready,
    )
    lax.fori_loop(done, chunks, wait, 0)


def side_kernel(
    dims, table, coeffs, gh, gh2, gs, gs2, occ, energy, atoms, before, *rest
):
    rims, acc, cells, sems = rest[:-3], rest[-3], rest[-2], rest[-1]
    copies, start = [], 0
    for k, rim in enumerate(rims):
        size = rim.shape[0]
        copies.append(pltpu.make_async_copy(rim, cells.at[pl.ds(start, size)], sems.at[k]))
        start += size
    for copy in copies:
        copy.start()
    acc[...] = before[...]
    for copy in copies:
        copy.wait()
    stage_body(
        dims, 1, lambda spot: cells[spot], table, coeffs, (gh, gh2, gs, gs2), occ, energy, atoms, acc,
    )


def low_kernel(
    dims, table, coeffs, gh, gh2, gs, gs2, occ, energy, atoms, before, rim, acc
):
    acc[...] = before[...]
    stage_body(
        dims, 2, lambda spot: rim[spot], table, coeffs, (gh, gh2, gs, gs2), occ, energy, atoms, acc
    )


def last_kernel(
    dims, table, coeffs, gh, gh2, gs, gs2, occ, energy, atoms, before, *rest
):
    rims, out, acc = rest[:-2], rest[-2], rest[-1]
    acc[...] = before[...]

    def right(spot):
        start, cell = 0, None
        for rim in rims:
            size = rim.shape[0]
            here = rim[jnp.clip(spot - start, 0, size - 1)]
            cell = here if cell is None else jnp.where(spot >= start, here, cell)
            start += size
        return cell

    number = table[12 * dims[2] + 3]
    for group, chosen in ((GROUP, number <= GROUP), (OWN_GROUP, number > GROUP)):

        @pl.when(chosen)
        def _(group=group):
            stage_body(
                dims, 3, right, table, coeffs, (gh, gh2, gs, gs2), occ, energy, atoms, acc, group
            )

    basis = atoms.shape[1]
    for c in range(3):
        out[c] = -2.0 * jnp.sum(acc[:, :, c * basis : (c + 1) * basis], axis=2)


def per_device(
    coeffs, occupation, energies, row_atom, pair_first, pair_second, pair_count, deriv_h, deriv_s
):
    width_x, width_y, basis, columns = coeffs.shape
    half_rows = row_atom.shape[2]
    local = width_x * width_y
    slots = pair_first.shape[2]
    dims = (width_x, width_y, slots)

    grad_h = deriv_h.reshape(slots, 3, half_rows, basis)
    grad_s = deriv_s.reshape(slots, 3, half_rows, basis)
    grad_h_far, grad_s_far = shift(grad_h, "orb", 1), shift(grad_s, "orb", 1)
    low_edge = shift(coeffs[width_x - 1, :: width_y - 1], "cx", 1)
    high_edge = shift(coeffs[0, :: width_y - 1], "cx", -1)
    low_mid = shift(coeffs[width_x - 1, 1 : width_y - 1], "cx", 1)
    low_side = shift(after(coeffs[:, width_y - 1], low_edge), "cy", 1)
    high_side = shift(after(coeffs[:, 0], high_edge), "cy", -1)
    high_mid = shift(after(coeffs[0, 1 : width_y - 1], high_edge, low_edge), "cx", -1)
    low_corner = shift(jnp.stack((low_edge[1], high_edge[1])), "cy", 1)
    high_corner = shift(jnp.stack((low_edge[0], high_edge[0])), "cy", -1)

    half = lax.axis_index("orb")
    atoms_own = row_atom.reshape(local, half_rows)
    atoms_all = lax.all_gather(atoms_own, "orb", axis=0)
    atoms = jnp.concatenate(
        (atoms_own, jnp.where(half == 0, atoms_all[1], atoms_all[0])), axis=1
    )

    flat = coeffs.reshape(local, basis, columns)
    first, second = pair_first.reshape(slots), pair_second.reshape(slots)
    meta = jnp.stack((pair_count.reshape(()), half.astype(jnp.int32)))
    occ, energy = occupation.reshape(1, columns), energies.reshape(1, columns)

    acc_shape = jax.ShapeDtypeStruct((local, ATOMS, 3 * basis), jnp.float32)
    params = pltpu.CompilerParams(vmem_limit_bytes=6 * 1024 * 1024)

    def cost(share):
        pairs = int(slots * share)
        return pl.CostEstimate(
            flops=pairs * basis * 2 * basis * columns * 2,
            bytes_accessed=pairs * 2 * (2 * basis * columns + 6 * basis * basis),
            transcendentals=0,
        )

    table, atoms = pl.pallas_call(
        functools.partial(sort_kernel, dims),
        out_shape=(
            jax.ShapeDtypeStruct((12 * slots + 8,), jnp.int32),
            jax.ShapeDtypeStruct(atoms.shape, atoms.dtype),
        ),
        in_specs=[SMEM] * 4 + [VMEM] * 3,
        out_specs=(SMEM, VMEM),
        compiler_params=pltpu.CompilerParams(vmem_limit_bytes=12 * 1024 * 1024),
    )(first, second, meta, places_of(dims), atoms, flat, grad_s)
    acc, grad_h2, grad_s2 = pl.pallas_call(
        functools.partial(own_kernel, dims),
        out_shape=(
            acc_shape,
            jax.ShapeDtypeStruct(grad_h.shape, grad_h.dtype),
            jax.ShapeDtypeStruct(grad_s.shape, grad_s.dtype),
        ),
        in_specs=[SMEM] + [VMEM] * 3 + [ANY] * 2 + [VMEM] * 3,
        out_specs=(VMEM, VMEM, VMEM),
        scratch_shapes=[pltpu.SemaphoreType.DMA((slots // CHUNK, 2))],
        compiler_params=params,
        cost_estimate=cost(0.75),
    )(table, flat, grad_h, grad_s, grad_h_far, grad_s_far, occ, energy, atoms)
    common = (table, flat, grad_h, grad_h2, grad_s, grad_s2, occ, energy, atoms)
    common_specs = [SMEM] + [VMEM] * 8
    rims = (low_side, high_side, low_edge, high_edge)
    acc = pl.pallas_call(
        functools.partial(side_kernel, dims),
        out_shape=acc_shape,
        in_specs=common_specs + [VMEM] * (1 + len(rims)),
        out_specs=VMEM,
        scratch_shapes=[
            pltpu.VMEM((sum(rim.shape[0] for rim in rims), basis, columns), jnp.bfloat16),
            pltpu.SemaphoreType.DMA((len(rims),)),
        ],
        compiler_params=params,
        cost_estimate=cost(0.15),
    )(*common, acc, *rims)
    acc = pl.pallas_call(
        functools.partial(low_kernel, dims),
        out_shape=acc_shape,
        in_specs=common_specs + [VMEM] * 2,
        out_specs=VMEM,
        compiler_params=params,
        cost_estimate=cost(0.1),
    )(*common, acc, low_mid)
    out = pl.pallas_call(
        functools.partial(last_kernel, dims),
        out_shape=jax.ShapeDtypeStruct((3, local, ATOMS), jnp.float32),
        in_specs=common_specs + [VMEM] * 4,
        out_specs=VMEM,
        scratch_shapes=[pltpu.VMEM(acc_shape.shape, jnp.float32)],
        compiler_params=params,
        cost_estimate=cost(0.1),
    )(*common, acc, high_mid, low_corner, high_corner)
    total = out + shift(out, "orb", 1)
    return total.reshape(3, width_x, width_y, ATOMS)


def solution(mesh):
    return jax.shard_map(
        per_device,
        mesh=mesh,
        in_specs=(
            P("cx", "cy", None, "orb"),
            P("orb"),
            P("orb"),
            P("cx", "cy", "orb"),
            P("cx", "cy", None),
            P("cx", "cy", None),
            P("cx", "cy"),
            P("cx", "cy", None, None, "orb", None),
            P("cx", "cy", None, None, "orb", None),
        ),
        out_specs=P(None, "cx", "cy", None),
        check_vma=False,
    )
```
